32 devices in a mesh: gx: 8 (over z, y), gy: 4 (over x, core).
Axes of the slice: x: 2, y: 2, z: 4, core: 2. Of those that a mesh axis runs over, the one named last changes fastest.
Arguments:
- pressure: float32 [32, 256, 128], P('gx', 'gy'), may hold values from 0.5 to 2
- sat_water: float32 [32, 256, 128], P('gx', 'gy'), may hold values from 0.15 to 0.45
- sat_gas: float32 [32, 256, 128], P('gx', 'gy'), may hold values from 0.05 to 0.35
- pore_volume: float32 [32, 256, 128], P('gx', 'gy'), may hold values from 0.05 to 0.5
- mass_old: float32 [3, 32, 256, 128], P(None, 'gx', 'gy'), may hold values from -1.5 to 1.5
- transmissibility: float32 [3, 32, 256, 128], P(None, 'gx', 'gy'), may hold values from 0.1 to 3
- upwind: int32 [3, 3, 32, 256, 128], P(None, None, 'gx', 'gy'), may hold values from 0 to 1
Outputs:
- residual: float32 [3, 32, 256, 128], P(None, 'gx', 'gy')
- diag_block: float32 [9, 32, 256, 128], P(None, 'gx', 'gy')
- lower_block: float32 [3, 9, 32, 256, 128], P(None, None, 'gx', 'gy')
- upper_block: float32 [3, 9, 32, 256, 128], P(None, None, 'gx', 'gy')
- pressure_rows: float32 [7, 32, 256, 128], P(None, 'gx', 'gy')
- prolongator: float32 [7, 32, 256, 128], P(None, 'gx', 'gy')
- coarse_rhs: float32 [16, 128, 128], P('gx', 'gy')
The draws below stay inside these ranges and needn't reach their ends.
All inputs are finite; a program needn't handle non-finite values.
Results may differ from the reference program's by a relative error of at most 0.0001.
Values sent between devices are 32-bit elements; how exact they have to be, the bound alone decides.
A program may use at most 64 MiB of HBM per device.

```python
import math
import jax
import jax.numpy as jnp
from jax import lax

NZ = 128
NX = 32
NY = 256


def touch_ends(values, key, smallest, largest):
    longest = values.shape.index(max(values.shape))
    spots = []
    for shift in (0, 1):
        where = [jax.random.randint(jax.random.fold_in(key, axis), (), 0, length) for axis, length in enumerate(values.shape)]
        where[longest] = (where[longest] + shift) % values.shape[longest]
        spots.append(tuple(where))
    return values.at[spots[0]].set(smallest).at[spots[1]].set(largest)


def level_of(own_key, extent, shards, least, largest):
    loudness = 1.0
    for position, parts in shards:
        draws = jax.random.uniform(jax.random.fold_in(jax.random.fold_in(own_key, 6), position), (parts,), jnp.float32, least / len(shards), largest / len(shards))
        loudness = loudness * jnp.repeat(jnp.exp(draws), extent[position] // parts).reshape((-1,) + (1,) * (len(extent) - 1 - position))
    return loudness


def centred(stream_key, extent, spread, most, split=(), kind=jnp.bfloat16):
    values = jax.random.normal(stream_key, extent, jnp.float32) * spread
    if len(split) > 0:
        values = level_of(stream_key, extent, split, -0.22, 0.18) * values
    return jnp.clip(values, min=-most, max=most).astype(kind)


def setup_inputs(seed: int = 0) -> dict:
    key_of = jax.random.split(jax.random.key(seed), 8)
    pressure = jnp.clip(0.5 + 1.5 * jax.random.uniform(key_of[0], (NX, NY, NZ), jnp.float32) ** level_of(key_of[0], (NX, NY, NZ), ((0, 8), (1, 4)), -0.2, 0.2), 0.5, 2.0)
    sat_water = jnp.clip(0.15 + 0.29999998 * jax.random.uniform(key_of[1], (NX, NY, NZ), jnp.float32) ** level_of(key_of[1], (NX, NY, NZ), ((0, 8), (1, 4)), -0.2, 0.2), 0.15, 0.45)
    sat_gas = jnp.clip(0.05 + 0.29999999 * jax.random.uniform(key_of[2], (NX, NY, NZ), jnp.float32) ** level_of(key_of[2], (NX, NY, NZ), ((0, 8), (1, 4)), -0.2, 0.2), 0.05, 0.35)
    pore_volume = jnp.clip(jnp.exp(math.log(0.5) - 2.3025851 * jax.random.uniform(key_of[3], (NX, NY, NZ), jnp.float32) ** level_of(key_of[3], (NX, NY, NZ), ((0, 8), (1, 4)), -0.2, 0.2)), 0.05, 0.5)
    mass_old = centred(key_of[4], (3, NX, NY, NZ), 0.1, 1.5, ((1, 8), (2, 4)), jnp.float32)
    transmissibility = jnp.clip(jnp.exp(math.log(3.0) - 3.4011974 * jax.random.uniform(key_of[5], (3, NX, NY, NZ), jnp.float32) ** level_of(key_of[5], (3, NX, NY, NZ), ((1, 8), (2, 4)), -0.2, 0.2)), 0.1, 3.0)
    upwind = touch_ends(jax.random.randint(key_of[6], (3, 3, NX, NY, NZ), 0, 2), jax.random.fold_in(key_of[6], 1), 0, 1).astype(jnp.int32)
    return {"pressure": pressure, "sat_water": sat_water, "sat_gas": sat_gas, "pore_volume": pore_volume, "mass_old": mass_old, "transmissibility": transmissibility, "upwind": upwind}


comp_water = 0.05
comp_oil = 0.1
rock_comp = 0.02
gas_ratio = 0.3
visc_water = 0.5
visc_oil = 2.0
visc_gas = 0.2
head_flat = (0.0, 0.0, 0.0)
head_depth = (0.1, 0.08, 0.02)
time_step = 0.5
damping = 2.0 / 3.0

def volumes(states):
    press = states[0]
    water = states[1]
    gas_sat = states[2]
    oil_sat = 1.0 - water - gas_sat
    b_water = 1.0 + comp_water * press
    b_oil = 1.0 + comp_oil * press
    return (press, water, gas_sat, oil_sat, b_water, b_oil, press)

def mobility(states):
    press, water, gas_sat, oil_sat, b_water, b_oil, b_gas = volumes(states)
    moving = jnp.stack([water * water * b_water / visc_water, oil_sat * oil_sat * b_oil / visc_oil, gas_sat * gas_sat * b_gas / visc_gas])
    return (moving, gas_ratio * press)

def face_flux(lower_state, upper_state, trans, upwind, head):
    mob_lower, solved_lower = mobility(lower_state)
    mob_upper, solved_upper = mobility(upper_state)
    chosen = upwind * mob_lower + (1.0 - upwind) * mob_upper
    drop = lower_state[0] - upper_state[0]
    heads = jnp.array(head, jnp.float32).reshape(3, 1, 1, 1)
    phases = trans[None] * chosen * (drop[None] + heads)
    solved = upwind[1] * solved_lower + (1.0 - upwind[1]) * solved_upper
    return jnp.stack([phases[0], phases[1], phases[2] + solved * phases[1]])

def unit_rows(template):
    return [jnp.stack([jnp.ones_like(template[0]) if column == row else jnp.zeros_like(template[0]) for column in range(3)]) for row in range(3)]

def face_terms(lower_state, upper_state, trans, upwind, head):
    fluxes, pullback = jax.vjp(lambda first, second: face_flux(first, second, trans, upwind, head), lower_state, upper_state)
    by_lower = []
    by_upper = []
    for cotangent in unit_rows(fluxes):
        wrt_lower, wrt_upper = pullback(cotangent)
        by_lower.append(wrt_lower)
        by_upper.append(wrt_upper)
    return (fluxes, jnp.concatenate(by_lower, 0), jnp.concatenate(by_upper, 0))

def accumulate(states, pore_volume):
    press, water, gas_sat, oil_sat, b_water, b_oil, b_gas = volumes(states)
    porosity = pore_volume * (1.0 + rock_comp * press)
    return jnp.stack([porosity * b_water * water, porosity * b_oil * oil_sat, porosity * (b_gas * gas_sat + gas_ratio * press * b_oil * oil_sat)])

def accumulation_terms(states, pore_volume):
    masses, pullback = jax.vjp(lambda first: accumulate(first, pore_volume), states)
    rows = [pullback(cotangent)[0] for cotangent in unit_rows(masses)]
    return (masses, jnp.concatenate(rows, 0))

def impes_weights(states):
    press, water, gas_sat, oil_sat, b_water, b_oil, b_gas = volumes(states)
    return jnp.stack([1.0 / b_water, 1.0 / b_oil - gas_ratio, 1.0 / b_gas])

def cut_layer(field, dimension, first_index, last_index):
    return lax.slice_in_dim(field, first_index, last_index, axis=dimension)

def raise_up(field, upper_face, dimension):
    count = field.shape[dimension]
    return jnp.concatenate([cut_layer(field, dimension, 1, count), upper_face], dimension)

def sink_down(field, lower_face, dimension):
    count = field.shape[dimension]
    return jnp.concatenate([lower_face, cut_layer(field, dimension, 0, count - 1)], dimension)

def face_field(states, below, dimension, start, trans, upwind, head):
    lower_state = sink_down(states, below, dimension)
    positions = start + lax.broadcasted_iota(jnp.int32, trans.shape, dimension - 1)
    trans_live = jnp.where(positions > 0, trans, jnp.zeros_like(trans))
    return face_terms(lower_state, states, trans_live, upwind, head)

def assemble(masses, acc_block, mass_old, faces_all, tops_all):
    residual = (masses - mass_old) / time_step
    diagonal = acc_block / time_step
    lowers = []
    uppers = []
    for direction in range(3):
        fluxes, by_lower, by_upper = faces_all[direction]
        flux_top, lower_top, upper_top = tops_all[direction]
        dimension = direction + 1
        residual = residual - fluxes + raise_up(fluxes, flux_top, dimension)
        diagonal = diagonal - by_upper + raise_up(by_lower, lower_top, dimension)
        lowers.append(-by_lower)
        uppers.append(raise_up(by_upper, upper_top, dimension))
    return (residual, diagonal, lowers, uppers)

def pressure_section(weight, acc_block, diagonal, lowers, uppers, odd_x, odd_y):

    def column(block):
        return lax.optimization_barrier(jnp.sum(weight * block[0::3], axis=0))
    press_diag = column(diagonal)
    press_lower = [column(block) for block in lowers]
    press_upper = [column(block) for block in uppers]
    accum = column(acc_block) / time_step
    divisor = jnp.abs(press_diag) + accum
    for entry in press_lower + press_upper:
        divisor = divisor + jnp.abs(entry)
    scale = damping / divisor
    nothing = jnp.zeros_like(odd_x)
    same_lower = [odd_x, odd_y, nothing]
    same_upper = [1.0 - odd_x, 1.0 - odd_y, nothing]
    inside = press_diag
    for direction in range(3):
        inside = inside + same_lower[direction] * press_lower[direction] + same_upper[direction] * press_upper[direction]
    own_weight = 1.0 - scale * inside
    near_lower = [-scale * press_lower[direction] * (1.0 - same_lower[direction]) for direction in range(3)]
    near_upper = [-scale * press_upper[direction] * (1.0 - same_upper[direction]) for direction in range(3)]
    rows_out = jnp.stack([press_diag] + press_lower + press_upper)
    prolong = jnp.stack([own_weight] + near_lower + near_upper)
    return (rows_out, prolong)

def contributions(prolong, residual, weight):
    reduced = lax.optimization_barrier(jnp.sum(weight * residual, axis=0))
    shares = prolong * reduced[None]
    layer_z = jnp.zeros_like(reduced[:, :, 0:1])
    local_sum = shares[0] + raise_up(shares[3], layer_z, 2) + sink_down(shares[6], layer_z, 2)
    sideways = jnp.stack([shares[1], shares[4], shares[2], shares[5]])
    return (local_sum, sideways)

def block_sum(field):
    span_a, span_b, span_c = field.shape[-3:]
    shaped = field.reshape(field.shape[:-3] + (span_a // 2, 2, span_b // 2, 2, span_c))
    return lax.optimization_barrier(jnp.sum(shaped, axis=(-4, -2)))

def reference(pressure, sat_water, sat_gas, pore_volume, mass_old, transmissibility, upwind):
    states = jnp.stack([pressure, sat_water, sat_gas])
    masses, acc_block = accumulation_terms(states, pore_volume)
    weight = impes_weights(states)
    flags = upwind.astype(jnp.float32)
    faces_all = []
    tops_all = []
    for direction in range(3):
        dimension = direction + 1
        below = jnp.zeros_like(cut_layer(states, dimension, 0, 1))
        head = head_depth if direction == 2 else head_flat
        faces_all.append(face_field(states, below, dimension, 0, transmissibility[direction], flags[direction], head))
        zero_nine = jnp.zeros_like(cut_layer(acc_block, dimension, 0, 1))
        tops_all.append((below, zero_nine, zero_nine))
    residual, diagonal, lowers, uppers = assemble(masses, acc_block, mass_old, faces_all, tops_all)
    odd_x = (lax.broadcasted_iota(jnp.int32, pressure.shape, 0) % 2).astype(jnp.float32)
    odd_y = (lax.broadcasted_iota(jnp.int32, pressure.shape, 1) % 2).astype(jnp.float32)
    rows_out, prolong = pressure_section(weight, acc_block, diagonal, lowers, uppers, odd_x, odd_y)
    local_sum, sideways = contributions(prolong, residual, weight)
    edge_x = jnp.zeros_like(local_sum[0:1])
    edge_y = jnp.zeros_like(local_sum[:, 0:1])
    total = local_sum + raise_up(sideways[0], edge_x, 0) + sink_down(sideways[1], edge_x, 0)
    total = total + raise_up(sideways[2], edge_y, 1) + sink_down(sideways[3], edge_y, 1)
    coarse = block_sum(total)
    return (residual, diagonal, jnp.stack(lowers), jnp.stack(uppers), rows_out, prolong, coarse)
```

```python
import jax
import jax.numpy as jnp
from jax import lax
from jax.experimental import pallas as pl
from jax.experimental.pallas import tpu as pltpu
from jax.sharding import PartitionSpec as P

MESH = pl.DeviceIdType.MESH
ROWS = 8
PLACES = (0, 1, 3, 4, 6, 7, 8)


def neighbours():
    found = []
    for axis in ("gx", "gy"):
        here, size = lax.axis_index(axis), lax.axis_size(axis)
        found.append((axis, here - 1, here > 0))
        found.append((axis, here + 1, here < size - 1))
    return found


def meet():
    barrier = pltpu.get_barrier_semaphore()
    for axis, other, there in neighbours():

        @pl.when(there)
        def _():
            pl.semaphore_signal(barrier, inc=1, device_id={axis: other}, device_id_type=MESH)

    peers = sum(there.astype(jnp.int32) for _, _, there in neighbours())
    pl.semaphore_wait(barrier, peers)


def halo_kernel(p, sw, sg, t, u, xlo, xhi, xt, xu, ylo, yhi, yt, yu, send, recv):
    nx, ny, nz = p.shape
    states = (p, sw, sg)
    last = pl.ds(ny - ROWS, ROWS)
    first = pl.ds(0, ROWS)
    x_up = [(s.at[nx - 1], xlo.at[i]) for i, s in enumerate(states)]
    x_down = [(s.at[0], xhi.at[i]) for i, s in enumerate(states)]
    x_down += [(t.at[0, 0], xt), (u.at[0, :, 0], xu)]
    y_up = [(s.at[:, last], ylo.at[i]) for i, s in enumerate(states)]
    y_down = [(s.at[:, first], yhi.at[i]) for i, s in enumerate(states)]
    y_down += [(t.at[1, :, first], yt), (u.at[1, :, :, first], yu)]
    groups = (x_down, x_up, y_down, y_up)
    (_, xl, has_xl), (_, xh, has_xh), (_, yl, has_yl), (_, yh, has_yh) = neighbours()
    routes = (
        ("gx", xl, has_xl, has_xh),
        ("gx", xh, has_xh, has_xl),
        ("gy", yl, has_yl, has_yh),
        ("gy", yh, has_yh, has_yl),
    )
    meet()
    remote = []
    index = 0
    for group, (axis, other, sends, gets) in zip(groups, routes):
        copies = []
        for source, target in group:
            copies.append(
                pltpu.make_async_remote_copy(
                    src_ref=source,
                    dst_ref=target,
                    send_sem=send.at[index],
                    recv_sem=recv.at[index],
                    device_id={axis: other},
                    device_id_type=MESH,
                )
            )
            index += 1
        remote.append(copies)

        @pl.when(sends)
        def _():
            for copy in copies:
                copy.start()

    index = 0
    for group, (axis, other, sends, gets) in zip(groups, routes):

        @pl.when(jnp.logical_not(gets))
        def _():
            for k, (source, target) in enumerate(group):
                pltpu.make_async_copy(source, target, recv.at[index + k]).start()
            for k, (source, target) in enumerate(group):
                pltpu.make_async_copy(source, target, recv.at[index + k]).wait()

        index += len(group)
    for copies, (axis, other, sends, gets) in zip(remote, routes):

        @pl.when(sends)
        def _():
            for copy in copies:
                copy.wait_send()

        @pl.when(gets)
        def _():
            for copy in copies:
                copy.wait_recv()


def cell(p, sw, sg):
    so = 1.0 - sw - sg
    bw = 1.0 + 0.05 * p
    bo = 1.0 + 0.1 * p
    ww, oo, gg = sw * sw, so * so, 5.0 * (sg * sg)
    sob = so * bo
    return dict(
        p=p, sw=sw, sg=sg, so=so, bw=bw, bo=bo, sob=sob, rs=0.3 * p,
        m=(2.0 * ww * bw, 0.5 * so * sob, gg * p),
        mp=(0.1 * ww, 0.05 * oo, gg),
        ms=(4.0 * sw * bw, -sob, 10.0 * sg * p),
    )


def face(low, high, t, flags, heads):
    drop = low["p"] - high["p"]
    ups = [flag > 0 for flag in flags]
    flow, by_low, by_high = [], [], []
    for a in range(3):
        drive = t * (drop + heads[a]) if heads[a] else t * drop
        chosen = jnp.where(ups[a], low["m"][a], high["m"][a])
        moved = t * chosen
        flow.append(drive * chosen)
        from_low = jnp.where(ups[a], drive, 0.0)
        from_high = jnp.where(ups[a], 0.0, drive)
        by_low.append((from_low * low["mp"][a] + moved, from_low * low["ms"][a]))
        by_high.append((from_high * high["mp"][a] - moved, from_high * high["ms"][a]))
    solved = jnp.where(ups[1], low["rs"], high["rs"])
    fluxes = [flow[0], flow[1], flow[2] + solved * flow[1]]
    third = 0.3 * flow[1]
    extra_low = jnp.where(ups[1], third, 0.0)
    extra_high = jnp.where(ups[1], 0.0, third)
    out = []
    for (w, o, g), extra in ((by_low, extra_low), (by_high, extra_high)):
        carried = solved * o[1]
        out.append([w[0], w[1], o[0], o[1], g[0] + solved * o[0] + extra, carried, g[1] + carried])
    return fluxes, out[0], out[1]


def column(weight, entries):
    return weight[0] * entries[0] + weight[1] * entries[2] + weight[2] * entries[4]


def put(ref, lead, x, rows, entries, sign=1.0):
    for place, entry in zip(PLACES, entries):
        ref[lead + (place, x, rows)] = entry if sign > 0 else -entry
    ref[lead + (2, x, rows)] = jnp.zeros_like(entries[0])
    ref[lead + (5, x, rows)] = entries[3] if sign > 0 else -entries[3]


def main_kernel(
    p, sw, sg, pv, old, t, u, xlo, xhi, xt, xu, ylo, yhi, yt, yu,
    res_o, diag_o, low_o, up_o, rows_o, pro_o, coarse_o, sx_o, sy_o,
    ps, pvs, olds, txs, tys, tzs, uxs, uys, uzs,
    res_v, diag_v, low_v, up_v, rows_v, pro_v, own_s, side_s,
    in_sem, out_sem,
):
    nx, ny, nz = p.shape
    steps = ny // ROWS
    inner = pl.ds(ROWS, ny)
    mid = pl.ds(1, nx)
    pairs = []
    for i, s in enumerate((p, sw, sg)):
        pairs += [
            (s, ps.at[i, mid, inner]),
            (xlo.at[i], ps.at[i, 0, inner]),
            (xhi.at[i], ps.at[i, nx + 1, inner]),
            (ylo.at[i], ps.at[i, mid, pl.ds(0, ROWS)]),
            (yhi.at[i], ps.at[i, mid, pl.ds(ROWS + ny, ROWS)]),
        ]
    pairs += [
        (pv, pvs), (old, olds),
        (t.at[0], txs.at[pl.ds(0, nx)]), (xt, txs.at[nx]),
        (t.at[1], tys.at[:, pl.ds(0, ny)]), (yt, tys.at[:, pl.ds(ny, ROWS)]),
        (t.at[2], tzs),
        (u.at[0], uxs.at[:, pl.ds(0, nx)]), (xu, uxs.at[:, nx]),
        (u.at[1], uys.at[:, :, pl.ds(0, ny)]), (yu, uys.at[:, :, pl.ds(ny, ROWS)]),
        (u.at[2], uzs),
    ]
    copies = [pltpu.make_async_copy(a, b, in_sem.at[k]) for k, (a, b) in enumerate(pairs)]
    for copy in copies:
        copy.start()
    for copy in copies:
        copy.wait()

    gx, gy = lax.axis_index("gx"), lax.axis_index("gy")

    @pl.when(gx == 0)
    def _():
        txs[0] = jnp.zeros((ny, nz), jnp.float32)

    @pl.when(gx == lax.axis_size("gx") - 1)
    def _():
        txs[nx] = jnp.zeros((ny, nz), jnp.float32)

    @pl.when(gy == 0)
    def _():
        tys[:, 0:1] = jnp.zeros((nx, 1, nz), jnp.float32)

    @pl.when(gy == lax.axis_size("gy") - 1)
    def _():
        tys[:, ny : ny + 1] = jnp.zeros((nx, 1, nz), jnp.float32)

    side_s[:, 0:ROWS] = jnp.zeros((nx // 2, ROWS, nz), jnp.float32)
    side_s[:, ny + ROWS :] = jnp.zeros((nx // 2, ROWS, nz), jnp.float32)

    lane = lax.broadcasted_iota(jnp.int32, (ROWS, nz), 1)
    odd = lax.broadcasted_iota(jnp.int32, (ROWS, nz), 0) % 2 == 1
    flat, depth = (0.0, 0.0, 0.0), (0.1, 0.08, 0.02)
    outs = ((res_v, res_o), (diag_v, diag_o), (low_v, low_o), (up_v, up_o), (rows_v, rows_o), (pro_v, pro_o))

    def out_copies(j):
        made = []
        rows = pl.ds(pl.multiple_of(j * ROWS, ROWS), ROWS)
        for k, (v, o) in enumerate(outs):
            lead = (slice(None),) * (len(v.shape) - 2)
            made.append(pltpu.make_async_copy(v.at[lead + (rows,)], o.at[lead + (rows,)], out_sem.at[j, k]))
        return made

    def step(j, carry):
        start = pl.multiple_of(j * ROWS, ROWS)
        rows = pl.ds(start, ROWS)
        here = pl.ds(pl.multiple_of(start + ROWS, ROWS), ROWS)
        before = pl.ds(start + ROWS - 1, ROWS)
        after = pl.ds(start + ROWS + 1, ROWS)
        following = pl.ds(start + 1, ROWS)

        def states(x, where):
            return [ps[i, x, where] for i in range(3)]

        def x_face(x, low, high):
            return face(low, high, txs[x, rows], [uxs[a, x, rows] for a in range(3)], flat)

        below, centre = cell(*states(0, here)), cell(*states(1, here))
        x_low = x_face(0, below, centre)
        agg = [None] * (nx // 2)
        side = [None] * (nx // 2)

        def add(items, place, value):
            items[place] = value if items[place] is None else items[place] + value

        for x in range(nx):
            above = cell(*states(x + 2, here))
            x_up = x_face(x + 1, centre, above)
            y_low = face(
                cell(*states(x + 1, before)), centre, tys[x, rows],
                [uys[a, x, rows] for a in range(3)], flat,
            )
            y_up = face(
                centre, cell(*states(x + 1, after)), tys[x, following],
                [uys[a, x, following] for a in range(3)], flat,
            )
            under = cell(*[pltpu.roll(centre[n], 1, 1) for n in ("p", "sw", "sg")])
            z_t = jnp.where(lane > 0, tzs[x, rows], 0.0)
            z_low = face(under, centre, z_t, [uzs[a, x, rows] for a in range(3)], depth)
            z_up = [[pltpu.roll(v, nz - 1, 1) for v in part] for part in z_low]
            lows, ups = (x_low, y_low, z_low), (x_up, y_up, z_up)

            c = centre
            pore = pvs[x, rows]
            phi = pore + 0.02 * pore * c["p"]
            dphi = 0.02 * pore
            water, oil = c["bw"] * c["sw"], c["sob"]
            gas = c["p"] * c["sg"] + c["rs"] * oil
            pob = phi * c["bo"]
            rob = c["rs"] * pob
            acc = [
                dphi * water + 0.05 * phi * c["sw"],
                phi * c["bw"],
                dphi * oil + 0.1 * phi * c["so"],
                -pob,
                dphi * gas + phi * (c["sg"] + 0.3 * oil + 0.1 * c["rs"] * c["so"]),
                -rob,
                phi * c["p"] - rob,
            ]
            acc = [2.0 * v for v in acc]
            mass = (phi * water, phi * oil, phi * gas)
            residual = []
            for k in range(3):
                r = 2.0 * (mass[k] - olds[k, x, rows])
                for d in range(3):
                    r = r - lows[d][0][k] + ups[d][0][k]
                res_v[k, x, rows] = r
                residual.append(r)
            diag = []
            for k in range(7):
                v = acc[k]
                for d in range(3):
                    v = v - lows[d][2][k] + ups[d][1][k]
                diag.append(v)
            put(diag_v, (), x, rows, diag)
            for d in range(3):
                put(low_v, (d,), x, rows, lows[d][1], -1.0)
                put(up_v, (d,), x, rows, ups[d][2])

            weight = (1.0 / c["bw"], 1.0 / c["bo"] - 0.3, 1.0 / c["p"])
            p_diag = column(weight, diag)
            p_low = [-column(weight, lows[d][1]) for d in range(3)]
            p_up = [column(weight, ups[d][2]) for d in range(3)]
            divisor = jnp.abs(p_diag) + column(weight, acc)
            for v in p_low + p_up:
                divisor = divisor + jnp.abs(v)
            scale = (2.0 / 3.0) / divisor
            for k, v in enumerate([p_diag] + p_low + p_up):
                rows_v[k, x, rows] = v
            y_same = jnp.where(odd, p_low[1], p_up[1])
            y_low_other = jnp.where(odd, 0.0, p_low[1])
            y_up_other = jnp.where(odd, p_up[1], 0.0)
            x_same, x_other = (p_low[0], p_up[0]) if x % 2 else (p_up[0], p_low[0])
            own = 1.0 - scale * (p_diag + x_same + y_same)
            minus = -scale
            w_x = minus * x_other
            w_yl, w_yu = minus * y_low_other, minus * y_up_other
            w_zl, w_zu = minus * p_low[2], minus * p_up[2]
            none = jnp.zeros_like(own)
            w_xl, w_xu = (none, w_x) if x % 2 else (w_x, none)
            for k, v in enumerate((own, w_xl, w_yl, w_zl, w_xu, w_yu, w_zu)):
                pro_v[k, x, rows] = v

            reduced = weight[0] * residual[0] + weight[1] * residual[1] + weight[2] * residual[2]
            local = own * reduced + pltpu.roll(w_zl * reduced, nz - 1, 1) + pltpu.roll(w_zu * reduced, 1, 1)
            add(agg, x // 2, local)
            add(side, x // 2, (w_yl + w_yu) * reduced)
            share = w_x * reduced
            if x == 0:
                own_s[nx // 2, rows] = share
            elif x == nx - 1:
                own_s[nx // 2 + 1, rows] = share
            else:
                add(agg, (x + 1) // 2 if x % 2 else (x - 1) // 2, share)
            x_low, centre = x_up, above
        for a in range(nx // 2):
            own_s[a, rows] = agg[a]
            side_s[a, here] = side[a]
        for copy in out_copies(j):
            copy.start()
        return carry

    lax.fori_loop(0, steps, step, 0)

    half = ny // 2
    for a in range(nx // 2):
        coarse_o[a] = (
            own_s[a, pl.ds(0, half, stride=2)]
            + own_s[a, pl.ds(1, half, stride=2)]
            + side_s[a, pl.ds(ROWS + 2, half, stride=2)]
            + side_s[a, pl.ds(ROWS - 1, half, stride=2)]
        )
        sy_o[0, a : a + 1] = side_s[a, ROWS : ROWS + 1]
        sy_o[1, a : a + 1] = side_s[a, ROWS + ny - 1 : ROWS + ny]
    for s in range(2):
        sx_o[s] = own_s[nx // 2 + s, pl.ds(0, half, stride=2)] + own_s[nx // 2 + s, pl.ds(1, half, stride=2)]

    def finish(j, carry):
        for copy in out_copies(j):
            copy.wait()
        return carry

    lax.fori_loop(0, steps, finish, 0)


def share_kernel(coarse, sx, sy, out, gx_in, gy_in, send, recv):
    ax, half, nz = coarse.shape
    (_, xl, has_xl), (_, xh, has_xh), (_, yl, has_yl), (_, yh, has_yh) = neighbours()
    meet()
    routes = (
        (sx.at[0], gx_in.at[0], "gx", xl, has_xl, has_xh),
        (sx.at[1], gx_in.at[1], "gx", xh, has_xh, has_xl),
        (sy.at[0], gy_in.at[0], "gy", yl, has_yl, has_yh),
        (sy.at[1], gy_in.at[1], "gy", yh, has_yh, has_yl),
    )
    copies = []
    for k, (source, target, axis, other, sends, gets) in enumerate(routes):
        copy = pltpu.make_async_remote_copy(
            src_ref=source, dst_ref=target, send_sem=send.at[k], recv_sem=recv.at[k],
            device_id={axis: other}, device_id_type=MESH,
        )
        copies.append(copy)

        @pl.when(sends)
        def _():
            copy.start()

    out[...] = coarse[...]
    for k, (source, target, axis, other, sends, gets) in enumerate(routes):
        copy = copies[k]

        @pl.when(gets)
        def _():
            copy.wait_recv()
            if k == 0:
                out[ax - 1] += gx_in[0]
            elif k == 1:
                out[0] += gx_in[1]
            else:
                place = half - 1 if k == 2 else 0
                for a in range(ax):
                    out[a, place : place + 1] += gy_in[k - 2, a : a + 1]

        @pl.when(sends)
        def _():
            copy.wait_send()


def body(pressure, sat_water, sat_gas, pore_volume, mass_old, transmissibility, upwind):
    nx, ny, nz = pressure.shape
    f32, i32 = jnp.float32, jnp.int32
    anywhere = pl.BlockSpec(memory_space=pl.ANY)
    in_vmem = pl.BlockSpec(memory_space=pltpu.VMEM)
    shape = jax.ShapeDtypeStruct
    halos = pl.pallas_call(
        halo_kernel,
        out_shape=[
            shape((3, ny, nz), f32), shape((3, ny, nz), f32), shape((ny, nz), f32), shape((3, ny, nz), i32),
            shape((3, nx, ROWS, nz), f32), shape((3, nx, ROWS, nz), f32), shape((nx, ROWS, nz), f32),
            shape((3, nx, ROWS, nz), i32),
        ],
        in_specs=[anywhere] * 5,
        out_specs=[anywhere] * 8,
        scratch_shapes=[pltpu.SemaphoreType.DMA((16,)), pltpu.SemaphoreType.DMA((16,))],
        compiler_params=pltpu.CompilerParams(collective_id=0, has_side_effects=True),
        name="halo",
    )(pressure, sat_water, sat_gas, transmissibility, upwind)
    grid = (nx, ny, nz)
    lead = ((3,), (9,), (3, 9), (3, 9), (7,), (7,))
    results = pl.pallas_call(
        main_kernel,
        out_shape=[shape(k + grid, f32) for k in lead]
        + [shape((nx // 2, ny // 2, nz), f32), shape((2, ny // 2, nz), f32), shape((2, nx // 2, nz), f32)],
        in_specs=[anywhere] * 15,
        out_specs=[anywhere] * 6 + [in_vmem] * 3,
        scratch_shapes=[
            pltpu.VMEM((3, nx + 2, ny + 2 * ROWS, nz), f32),
            pltpu.VMEM(grid, f32),
            pltpu.VMEM((3,) + grid, f32),
            pltpu.VMEM((nx + 1, ny, nz), f32),
            pltpu.VMEM((nx, ny + ROWS, nz), f32),
            pltpu.VMEM(grid, f32),
            pltpu.VMEM((3, nx + 1, ny, nz), i32),
            pltpu.VMEM((3, nx, ny + ROWS, nz), i32),
            pltpu.VMEM((3,) + grid, i32),
        ]
        + [pltpu.VMEM(k + grid, f32) for k in lead]
        + [
            pltpu.VMEM((nx // 2 + 2, ny, nz), f32),
            pltpu.VMEM((nx // 2, ny + 2 * ROWS, nz), f32),
            pltpu.SemaphoreType.DMA((27,)),
            pltpu.SemaphoreType.DMA((ny // ROWS, 6)),
        ],
        compiler_params=pltpu.CompilerParams(vmem_limit_bytes=40 * 2**20),
        name="assemble",
    )(pressure, sat_water, sat_gas, pore_volume, mass_old, transmissibility, upwind, *halos)
    *blocks, coarse, sx, sy = results
    coarse = pl.pallas_call(
        share_kernel,
        out_shape=shape(coarse.shape, f32),
        in_specs=[in_vmem] * 3,
        out_specs=in_vmem,
        scratch_shapes=[
            pltpu.VMEM(sx.shape, f32), pltpu.VMEM(sy.shape, f32),
            pltpu.SemaphoreType.DMA((4,)), pltpu.SemaphoreType.DMA((4,)),
        ],
        compiler_params=pltpu.CompilerParams(collective_id=1, has_side_effects=True),
        name="shares",
    )(coarse, sx, sy)
    return (*blocks, coarse)


def solution(mesh):
    cells = P("gx", "gy", None)
    one = P(None, "gx", "gy", None)
    two = P(None, None, "gx", "gy", None)
    return jax.shard_map(
        body,
        mesh=mesh,
        in_specs=(cells, cells, cells, cells, one, one, two),
        out_specs=(one, one, two, two, one, one, cells),
        check_vma=False,
    )
```

```python
import jax
import jax.numpy as jnp
from jax import lax
from jax.experimental import pallas as pl
from jax.experimental.pallas import tpu as pltpu
from jax.sharding import PartitionSpec as P

MESH = pl.DeviceIdType.MESH
ROWS = 8
PLACES = (0, 1, 3, 4, 6, 7, 8)


def neighbours():
    found = []
    for axis in ("gx", "gy"):
        here, size = lax.axis_index(axis), lax.axis_size(axis)
        found.append((axis, here - 1, here > 0))
        found.append((axis, here + 1, here < size - 1))
    return found


def meet():
    barrier = pltpu.get_barrier_semaphore()
    for axis, other, there in neighbours():

        @pl.when(there)
        def _():
            pl.semaphore_signal(barrier, inc=1, device_id={axis: other}, device_id_type=MESH)

    peers = sum(there.astype(jnp.int32) for _, _, there in neighbours())
    pl.semaphore_wait(barrier, peers)


def halo_kernel(p, sw, sg, t, u, xlo, xhi, xt, xu, ylo, yhi, yt, yu, send, recv):
    nx, ny, nz = p.shape
    states = (p, sw, sg)
    last = pl.ds(ny - ROWS, ROWS)
    first = pl.ds(0, ROWS)
    x_up = [(s.at[nx - 1], xlo.at[i]) for i, s in enumerate(states)]
    x_down = [(s.at[0], xhi.at[i]) for i, s in enumerate(states)]
    x_down += [(t.at[0, 0], xt), (u.at[0, :, 0], xu)]
    y_up = [(s.at[:, last], ylo.at[i]) for i, s in enumerate(states)]
    y_down = [(s.at[:, first], yhi.at[i]) for i, s in enumerate(states)]
    y_down += [(t.at[1, :, first], yt), (u.at[1, :, :, first], yu)]
    groups = (x_down, x_up, y_down, y_up)
    (_, xl, has_xl), (_, xh, has_xh), (_, yl, has_yl), (_, yh, has_yh) = neighbours()
    routes = (
        ("gx", xl, has_xl, has_xh),
        ("gx", xh, has_xh, has_xl),
        ("gy", yl, has_yl, has_yh),
        ("gy", yh, has_yh, has_yl),
    )
    meet()
    remote = []
    index = 0
    for group, (axis, other, sends, gets) in zip(groups, routes):
        copies = []
        for source, target in group:
            copies.append(
                pltpu.make_async_remote_copy(
                    src_ref=source,
                    dst_ref=target,
                    send_sem=send.at[index],
                    recv_sem=recv.at[index],
                    device_id={axis: other},
                    device_id_type=MESH,
                )
            )
            index += 1
        remote.append(copies)

        @pl.when(sends)
        def _():
            for copy in copies:
                copy.start()

    index = 0
    for group, (axis, other, sends, gets) in zip(groups, routes):

        @pl.when(jnp.logical_not(gets))
        def _():
            for k, (source, target) in enumerate(group):
                pltpu.make_async_copy(source, target, recv.at[index + k]).start()
            for k, (source, target) in enumerate(group):
                pltpu.make_async_copy(source, target, recv.at[index + k]).wait()

        index += len(group)
    for copies, (axis, other, sends, gets) in zip(remote, routes):

        @pl.when(sends)
        def _():
            for copy in copies:
                copy.wait_send()

        @pl.when(gets)
        def _():
            for copy in copies:
                copy.wait_recv()


def cell(p, sw, sg):
    so = 1.0 - sw - sg
    bw = 1.0 + 0.05 * p
    bo = 1.0 + 0.1 * p
    ww, oo, gg = sw * sw, so * so, 5.0 * (sg * sg)
    sob = so * bo
    return dict(
        p=p, sw=sw, sg=sg, so=so, bw=bw, bo=bo, sob=sob, rs=0.3 * p,
        m=(2.0 * ww * bw, 0.5 * so * sob, gg * p),
        mp=(0.1 * ww, 0.05 * oo, gg),
        ms=(4.0 * sw * bw, -sob, 10.0 * sg * p),
    )


def face(low, high, t, flags, heads):
    drop = low["p"] - high["p"]
    ups = [flag > 0 for flag in flags]
    flow, by_low, by_high = [], [], []
    for a in range(3):
        drive = t * (drop + heads[a]) if heads[a] else t * drop
        chosen = jnp.where(ups[a], low["m"][a], high["m"][a])
        moved = t * chosen
        flow.append(drive * chosen)
        from_low = jnp.where(ups[a], drive, 0.0)
        from_high = jnp.where(ups[a], 0.0, drive)
        by_low.append((from_low * low["mp"][a] + moved, from_low * low["ms"][a]))
        by_high.append((from_high * high["mp"][a] - moved, from_high * high["ms"][a]))
    solved = jnp.where(ups[1], low["rs"], high["rs"])
    fluxes = [flow[0], flow[1], flow[2] + solved * flow[1]]
    third = 0.3 * flow[1]
    extra_low = jnp.where(ups[1], third, 0.0)
    extra_high = jnp.where(ups[1], 0.0, third)
    out = []
    for (w, o, g), extra in ((by_low, extra_low), (by_high, extra_high)):
        carried = solved * o[1]
        out.append([w[0], w[1], o[0], o[1], g[0] + solved * o[0] + extra, carried, g[1] + carried])
    return fluxes, out[0], out[1]


def column(weight, entries):
    return weight[0] * entries[0] + weight[1] * entries[2] + weight[2] * entries[4]


def put(ref, lead, x, rows, entries, sign=1.0):
    for place, entry in zip(PLACES, entries):
        ref[lead + (place, x, rows)] = entry if sign > 0 else -entry
    ref[lead + (2, x, rows)] = jnp.zeros_like(entries[0])
    ref[lead + (5, x, rows)] = entries[3] if sign > 0 else -entries[3]


def main_kernel(
    p, sw, sg, pv, old, t, u, xlo, xhi, xt, xu, ylo, yhi, yt, yu,
    res_o, diag_o, low_o, up_o, rows_o, pro_o, coarse_o, sx_o, sy_o,
    ps, pvs, olds, txs, tys, tzs, uxs, uys, uzs,
    res_v, diag_v, low_v, up_v, rows_v, pro_v, own_s, side_s,
    in_sem, out_sem,
):
    nx, ny, nz = p.shape
    steps = ny // ROWS
    inner = pl.ds(ROWS, ny)
    mid = pl.ds(1, nx)
    pairs = []
    for i, s in enumerate((p, sw, sg)):
        pairs += [
            (s, ps.at[i, mid, inner]),
            (xlo.at[i], ps.at[i, 0, inner]),
            (xhi.at[i], ps.at[i, nx + 1, inner]),
            (ylo.at[i], ps.at[i, mid, pl.ds(0, ROWS)]),
            (yhi.at[i], ps.at[i, mid, pl.ds(ROWS + ny, ROWS)]),
        ]
    pairs += [
        (pv, pvs), (old, olds),
        (t.at[0], txs.at[pl.ds(0, nx)]), (xt, txs.at[nx]),
        (t.at[1], tys.at[:, pl.ds(0, ny)]), (yt, tys.at[:, pl.ds(ny, ROWS)]),
        (t.at[2], tzs),
        (u.at[0], uxs.at[:, pl.ds(0, nx)]), (xu, uxs.at[:, nx]),
        (u.at[1], uys.at[:, :, pl.ds(0, ny)]), (yu, uys.at[:, :, pl.ds(ny, ROWS)]),
        (u.at[2], uzs),
    ]
    copies = [pltpu.make_async_copy(a, b, in_sem.at[k]) for k, (a, b) in enumerate(pairs)]
    for copy in copies:
        copy.start()
    for copy in copies:
        copy.wait()

    gx, gy = lax.axis_index("gx"), lax.axis_index("gy")

    @pl.when(gx == 0)
    def _():
        txs[0] = jnp.zeros((ny, nz), jnp.float32)

    @pl.when(gx == lax.axis_size("gx") - 1)
    def _():
        txs[nx] = jnp.zeros((ny, nz), jnp.float32)

    @pl.when(gy == 0)
    def _():
        tys[:, 0:1] = jnp.zeros((nx, 1, nz), jnp.float32)

    @pl.when(gy == lax.axis_size("gy") - 1)
    def _():
        tys[:, ny : ny + 1] = jnp.zeros((nx, 1, nz), jnp.float32)

    side_s[:, 0:ROWS] = jnp.zeros((nx // 2, ROWS, nz), jnp.float32)
    side_s[:, ny + ROWS :] = jnp.zeros((nx // 2, ROWS, nz), jnp.float32)

    lane = lax.broadcasted_iota(jnp.int32, (ROWS, nz), 1)
    odd = lax.broadcasted_iota(jnp.int32, (ROWS, nz), 0) % 2 == 1
    flat, depth = (0.0, 0.0, 0.0), (0.1, 0.08, 0.02)
    outs = ((res_v, res_o), (diag_v, diag_o), (low_v, low_o), (up_v, up_o), (rows_v, rows_o), (pro_v, pro_o))

    def out_copies(j):
        made = []
        rows = pl.ds(pl.multiple_of(j * ROWS, ROWS), ROWS)
        for k, (v, o) in enumerate(outs):
            lead = (slice(None),) * (len(v.shape) - 2)
            made.append(pltpu.make_async_copy(v.at[lead + (rows,)], o.at[lead + (rows,)], out_sem.at[j, k]))
        return made

    def step(j, carry):
        start = pl.multiple_of(j * ROWS, ROWS)
        rows = pl.ds(start, ROWS)
        here = pl.ds(pl.multiple_of(start + ROWS, ROWS), ROWS)
        before = pl.ds(start + ROWS - 1, ROWS)
        after = pl.ds(start + ROWS + 1, ROWS)
        following = pl.ds(start + 1, ROWS)

        def states(x, where):
            return [ps[i, x, where] for i in range(3)]

        def x_face(x, low, high):
            return face(low, high, txs[x, rows], [uxs[a, x, rows] for a in range(3)], flat)

        below, centre = cell(*states(0, here)), cell(*states(1, here))
        x_low = x_face(0, below, centre)
        agg = [None] * (nx // 2)
        side = [None] * (nx // 2)

        def add(items, place, value):
            items[place] = value if items[place] is None else items[place] + value

        for x in range(nx):
            above = cell(*states(x + 2, here))
            x_up = x_face(x + 1, centre, above)
            y_low = face(
                cell(*states(x + 1, before)), centre, tys[x, rows],
                [uys[a, x, rows] for a in range(3)], flat,
            )
            y_up = face(
                centre, cell(*states(x + 1, after)), tys[x, following],
                [uys[a, x, following] for a in range(3)], flat,
            )
            under = cell(*[pltpu.roll(centre[n], 1, 1) for n in ("p", "sw", "sg")])
            z_t = jnp.where(lane > 0, tzs[x, rows], 0.0)
            z_low = face(under, centre, z_t, [uzs[a, x, rows] for a in range(3)], depth)
            z_up = [[pltpu.roll(v, nz - 1, 1) for v in part] for part in z_low]
            lows, ups = (x_low, y_low, z_low), (x_up, y_up, z_up)

            c = centre
            pore = pvs[x, rows]
            phi = pore + 0.02 * pore * c["p"]
            dphi = 0.02 * pore
            water, oil = c["bw"] * c["sw"], c["sob"]
            gas = c["p"] * c["sg"] + c["rs"] * oil
            pob = phi * c["bo"]
            rob = c["rs"] * pob
            acc = [
                dphi * water + 0.05 * phi * c["sw"],
                phi * c["bw"],
                dphi * oil + 0.1 * phi * c["so"],
                -pob,
                dphi * gas + phi * (c["sg"] + 0.3 * oil + 0.1 * c["rs"] * c["so"]),
                -rob,
                phi * c["p"] - rob,
            ]
            acc = [2.0 * v for v in acc]
            mass = (phi * water, phi * oil, phi * gas)
            residual = []
            for k in range(3):
                r = 2.0 * (mass[k] - olds[k, x, rows])
                for d in range(3):
                    r = r - lows[d][0][k] + ups[d][0][k]
                res_v[k, x, rows] = r
                residual.append(r)
            diag = []
            for k in range(7):
                v = acc[k]
                for d in range(3):
                    v = v - lows[d][2][k] + ups[d][1][k]
                diag.append(v)
            put(diag_v, (), x, rows, diag)
            for d in range(3):
                put(low_v, (d,), x, rows, lows[d][1], -1.0)
                put(up_v, (d,), x, rows, ups[d][2])

            weight = (1.0 / c["bw"], 1.0 / c["bo"] - 0.3, 1.0 / c["p"])
            p_diag = column(weight, diag)
            p_low = [-column(weight, lows[d][1]) for d in range(3)]
            p_up = [column(weight, ups[d][2]) for d in range(3)]
            divisor = jnp.abs(p_diag) + column(weight, acc)
            for v in p_low + p_up:
                divisor = divisor + jnp.abs(v)
            scale = (2.0 / 3.0) / divisor
            for k, v in enumerate([p_diag] + p_low + p_up):
                rows_v[k, x, rows] = v
            y_same = jnp.where(odd, p_low[1], p_up[1])
            y_low_other = jnp.where(odd, 0.0, p_low[1])
            y_up_other = jnp.where(odd, p_up[1], 0.0)
            x_same, x_other = (p_low[0], p_up[0]) if x % 2 else (p_up[0], p_low[0])
            own = 1.0 - scale * (p_diag + x_same + y_same)
            minus = -scale
            w_x = minus * x_other
            w_yl, w_yu = minus * y_low_other, minus * y_up_other
            w_zl, w_zu = minus * p_low[2], minus * p_up[2]
            none = jnp.zeros_like(own)
            w_xl, w_xu = (none, w_x) if x % 2 else (w_x, none)
            for k, v in enumerate((own, w_xl, w_yl, w_zl, w_xu, w_yu, w_zu)):
                pro_v[k, x, rows] = v

            reduced = weight[0] * residual[0] + weight[1] * residual[1] + weight[2] * residual[2]
            local = own * reduced + pltpu.roll(w_zl * reduced, nz - 1, 1) + pltpu.roll(w_zu * reduced, 1, 1)
            add(agg, x // 2, local)
            add(side, x // 2, (w_yl + w_yu) * reduced)
            share = w_x * reduced
            if x == 0:
                own_s[nx // 2, rows] = share
            elif x == nx - 1:
                own_s[nx // 2 + 1, rows] = share
            else:
                add(agg, (x + 1) // 2 if x % 2 else (x - 1) // 2, share)
            x_low, centre = x_up, above
        for a in range(nx // 2):
            own_s[a, rows] = agg[a]
            side_s[a, here] = side[a]
        for copy in out_copies(j):
            copy.start()
        return carry

    lax.fori_loop(0, steps, step, 0)

    half = ny // 2
    for a in range(nx // 2):
        coarse_o[a] = (
            own_s[a, pl.ds(0, half, stride=2)]
            + own_s[a, pl.ds(1, half, stride=2)]
            + side_s[a, pl.ds(ROWS + 2, half, stride=2)]
            + side_s[a, pl.ds(ROWS - 1, half, stride=2)]
        )
        sy_o[0, a : a + 1] = side_s[a, ROWS : ROWS + 1]
        sy_o[1, a : a + 1] = side_s[a, ROWS + ny - 1 : ROWS + ny]
    for s in range(2):
        sx_o[s] = own_s[nx // 2 + s, pl.ds(0, half, stride=2)] + own_s[nx // 2 + s, pl.ds(1, half, stride=2)]

    def finish(j, carry):
        for copy in out_copies(j):
            copy.wait()
        return carry

    lax.fori_loop(0, steps, finish, 0)


def share_kernel(coarse, sx, sy, out, gx_in, gy_in, send, recv):
    ax, half, nz = coarse.shape
    (_, xl, has_xl), (_, xh, has_xh), (_, yl, has_yl), (_, yh, has_yh) = neighbours()
    meet()
    routes = (
        (sx.at[0], gx_in.at[0], "gx", xl, has_xl, has_xh),
        (sx.at[1], gx_in.at[1], "gx", xh, has_xh, has_xl),
        (sy.at[0], gy_in.at[0], "gy", yl, has_yl, has_yh),
        (sy.at[1], gy_in.at[1], "gy", yh, has_yh, has_yl),
    )
    copies = []
    for k, (source, target, axis, other, sends, gets) in enumerate(routes):
        copy = pltpu.make_async_remote_copy(
            src_ref=source, dst_ref=target, send_sem=send.at[k], recv_sem=recv.at[k],
            device_id={axis: other}, device_id_type=MESH,
        )
        copies.append(copy)

        @pl.when(sends)
        def _():
            copy.start()

    out[...] = coarse[...]
    for k, (source, target, axis, other, sends, gets) in enumerate(routes):
        copy = copies[k]

        @pl.when(gets)
        def _():
            copy.wait_recv()
            if k == 0:
                out[ax - 1] += gx_in[0]
            elif k == 1:
                out[0] += gx_in[1]
            else:
                place = half - 1 if k == 2 else 0
                for a in range(ax):
                    out[a, place : place + 1] += gy_in[k - 2, a : a + 1]

        @pl.when(sends)
        def _():
            copy.wait_send()


def body(pressure, sat_water, sat_gas, pore_volume, mass_old, transmissibility, upwind):
    nx, ny, nz = pressure.shape
    f32, i32 = jnp.float32, jnp.int32
    anywhere = pl.BlockSpec(memory_space=pltpu.HBM)
    in_vmem = pl.BlockSpec(memory_space=pltpu.VMEM)
    shape = jax.ShapeDtypeStruct
    halos = pl.pallas_call(
        halo_kernel,
        out_shape=[
            shape((3, ny, nz), f32), shape((3, ny, nz), f32), shape((ny, nz), f32), shape((3, ny, nz), i32),
            shape((3, nx, ROWS, nz), f32), shape((3, nx, ROWS, nz), f32), shape((nx, ROWS, nz), f32),
            shape((3, nx, ROWS, nz), i32),
        ],
        in_specs=[anywhere] * 5,
        out_specs=[anywhere] * 8,
        scratch_shapes=[pltpu.SemaphoreType.DMA((16,)), pltpu.SemaphoreType.DMA((16,))],
        compiler_params=pltpu.CompilerParams(collective_id=0, has_side_effects=True),
        name="halo",
    )(pressure, sat_water, sat_gas, transmissibility, upwind)
    grid = (nx, ny, nz)
    lead = ((3,), (9,), (3, 9), (3, 9), (7,), (7,))
    results = pl.pallas_call(
        main_kernel,
        out_shape=[shape(k + grid, f32) for k in lead]
        + [shape((nx // 2, ny // 2, nz), f32), shape((2, ny // 2, nz), f32), shape((2, nx // 2, nz), f32)],
        in_specs=[anywhere] * 15,
        out_specs=[anywhere] * 6 + [in_vmem] * 3,
        scratch_shapes=[
            pltpu.VMEM((3, nx + 2, ny + 2 * ROWS, nz), f32),
            pltpu.VMEM(grid, f32),
            pltpu.VMEM((3,) + grid, f32),
            pltpu.VMEM((nx + 1, ny, nz), f32),
            pltpu.VMEM((nx, ny + ROWS, nz), f32),
            pltpu.VMEM(grid, f32),
            pltpu.VMEM((3, nx + 1, ny, nz), i32),
            pltpu.VMEM((3, nx, ny + ROWS, nz), i32),
            pltpu.VMEM((3,) + grid, i32),
        ]
        + [pltpu.VMEM(k + grid, f32) for k in lead]
        + [
            pltpu.VMEM((nx // 2 + 2, ny, nz), f32),
            pltpu.VMEM((nx // 2, ny + 2 * ROWS, nz), f32),
            pltpu.SemaphoreType.DMA((27,)),
            pltpu.SemaphoreType.DMA((ny // ROWS, 6)),
        ],
        compiler_params=pltpu.CompilerParams(vmem_limit_bytes=40 * 2**20),
        name="assemble",
    )(pressure, sat_water, sat_gas, pore_volume, mass_old, transmissibility, upwind, *halos)
    *blocks, coarse, sx, sy = results
    coarse = pl.pallas_call(
        share_kernel,
        out_shape=shape(coarse.shape, f32),
        in_specs=[in_vmem] * 3,
        out_specs=in_vmem,
        scratch_shapes=[
            pltpu.VMEM(sx.shape, f32), pltpu.VMEM(sy.shape, f32),
            pltpu.SemaphoreType.DMA((4,)), pltpu.SemaphoreType.DMA((4,)),
        ],
        compiler_params=pltpu.CompilerParams(collective_id=1, has_side_effects=True),
        name="shares",
    )(coarse, sx, sy)
    return (*blocks, coarse)


def solution(mesh):
    cells = P("gx", "gy", None)
    one = P(None, "gx", "gy", None)
    two = P(None, None, "gx", "gy", None)
    return jax.shard_map(
        body,
        mesh=mesh,
        in_specs=(cells, cells, cells, cells, one, one, two),
        out_specs=(one, one, two, two, one, one, cells),
        check_vma=False,
    )
```

```python
import jax
import jax.numpy as jnp
from jax import lax
from jax.experimental import pallas as pl
from jax.experimental.pallas import tpu as pltpu
from jax.sharding import PartitionSpec as P

MESH = pl.DeviceIdType.MESH
ROWS = 8
PLACES = (0, 1, 3, 4, 6, 7, 8)


def neighbours():
    found = []
    for axis in ("gx", "gy"):
        here, size = lax.axis_index(axis), lax.axis_size(axis)
        found.append((axis, here - 1, here > 0))
        found.append((axis, here + 1, here < size - 1))
    return found


def meet():
    barrier = pltpu.get_barrier_semaphore()
    for axis, other, there in neighbours():

        @pl.when(there)
        def _():
            pl.semaphore_signal(barrier, inc=1, device_id={axis: other}, device_id_type=MESH)

    peers = sum(there.astype(jnp.int32) for _, _, there in neighbours())
    pl.semaphore_wait(barrier, peers)


def halo_kernel(p, sw, sg, t, u, xlo, xhi, xt, xu, ylo, yhi, yt, yu, send, recv):
    nx, ny, nz = p.shape
    states = (p, sw, sg)
    last = pl.ds(ny - ROWS, ROWS)
    first = pl.ds(0, ROWS)
    x_up = [(s.at[nx - 1], xlo.at[i]) for i, s in enumerate(states)]
    x_down = [(s.at[0], xhi.at[i]) for i, s in enumerate(states)]
    x_down += [(t.at[0, 0], xt), (u.at[0, :, 0], xu)]
    y_up = [(s.at[:, last], ylo.at[i]) for i, s in enumerate(states)]
    y_down = [(s.at[:, first], yhi.at[i]) for i, s in enumerate(states)]
    y_down += [(t.at[1, :, first], yt), (u.at[1, :, :, first], yu)]
    groups = (x_down, x_up, y_down, y_up)
    (_, xl, has_xl), (_, xh, has_xh), (_, yl, has_yl), (_, yh, has_yh) = neighbours()
    routes = (
        ("gx", xl, has_xl, has_xh),
        ("gx", xh, has_xh, has_xl),
        ("gy", yl, has_yl, has_yh),
        ("gy", yh, has_yh, has_yl),
    )
    meet()
    remote = []
    index = 0
    for group, (axis, other, sends, gets) in zip(groups, routes):
        copies = []
        for source, target in group:
            copies.append(
                pltpu.make_async_remote_copy(
                    src_ref=source,
                    dst_ref=target,
                    send_sem=send.at[index],
                    recv_sem=recv.at[index],
                    device_id={axis: other},
                    device_id_type=MESH,
                )
            )
            index += 1
        remote.append(copies)

        @pl.when(sends)
        def _():
            for copy in copies:
                copy.start()

    index = 0
    for group, (axis, other, sends, gets) in zip(groups, routes):

        @pl.when(jnp.logical_not(gets))
        def _():
            for k, (source, target) in enumerate(group):
                pltpu.make_async_copy(source, target, recv.at[index + k]).start()
            for k, (source, target) in enumerate(group):
                pltpu.make_async_copy(source, target, recv.at[index + k]).wait()

        index += len(group)
    for copies, (axis, other, sends, gets) in zip(remote, routes):

        @pl.when(sends)
        def _():
            for copy in copies:
                copy.wait_send()

        @pl.when(gets)
        def _():
            for copy in copies:
                copy.wait_recv()


def cell(p, sw, sg):
    so = 1.0 - sw - sg
    bw = 1.0 + 0.05 * p
    bo = 1.0 + 0.1 * p
    ww, oo, gg = sw * sw, so * so, 5.0 * (sg * sg)
    sob = so * bo
    return dict(
        p=p, sw=sw, sg=sg, so=so, bw=bw, bo=bo, sob=sob, rs=0.3 * p,
        m=(2.0 * ww * bw, 0.5 * so * sob, gg * p),
        mp=(0.1 * ww, 0.05 * oo, gg),
        ms=(4.0 * sw * bw, -sob, 10.0 * sg * p),
    )


def face(low, high, t, flags, heads):
    drop = low["p"] - high["p"]
    ups = [flag > 0 for flag in flags]
    flow, by_low, by_high = [], [], []
    for a in range(3):
        drive = t * (drop + heads[a]) if heads[a] else t * drop
        chosen = jnp.where(ups[a], low["m"][a], high["m"][a])
        moved = t * chosen
        flow.append(drive * chosen)
        from_low = jnp.where(ups[a], drive, 0.0)
        from_high = jnp.where(ups[a], 0.0, drive)
        by_low.append((from_low * low["mp"][a] + moved, from_low * low["ms"][a]))
        by_high.append((from_high * high["mp"][a] - moved, from_high * high["ms"][a]))
    solved = jnp.where(ups[1], low["rs"], high["rs"])
    fluxes = [flow[0], flow[1], flow[2] + solved * flow[1]]
    third = 0.3 * flow[1]
    extra_low = jnp.where(ups[1], third, 0.0)
    extra_high = jnp.where(ups[1], 0.0, third)
    out = []
    for (w, o, g), extra in ((by_low, extra_low), (by_high, extra_high)):
        carried = solved * o[1]
        out.append([w[0], w[1], o[0], o[1], g[0] + solved * o[0] + extra, carried, g[1] + carried])
    return fluxes, out[0], out[1]


def column(weight, entries):
    return weight[0] * entries[0] + weight[1] * entries[2] + weight[2] * entries[4]


def put(ref, lead, x, rows, entries, sign=1.0):
    for place, entry in zip(PLACES, entries):
        ref[lead + (place, x, rows)] = entry if sign > 0 else -entry
    ref[lead + (2, x, rows)] = jnp.zeros_like(entries[0])
    ref[lead + (5, x, rows)] = entries[3] if sign > 0 else -entries[3]


def main_kernel(
    p, sw, sg, pv, old, t, u, xlo, xhi, xt, xu, ylo, yhi, yt, yu,
    res_o, diag_o, low_o, up_o, rows_o, pro_o, coarse_o, sx_o, sy_o,
    ps, pvs, olds, txs, tys, tzs, uxs, uys, uzs,
    res_v, diag_v, low_v, up_v, rows_v, pro_v, own_s, side_s,
    in_sem, out_sem,
):
    nx, ny, nz = p.shape
    steps = ny // ROWS
    inner = pl.ds(ROWS, ny)
    mid = pl.ds(1, nx)
    pairs = []
    for i, s in enumerate((p, sw, sg)):
        pairs += [
            (s, ps.at[i, mid, inner]),
            (xlo.at[i], ps.at[i, 0, inner]),
            (xhi.at[i], ps.at[i, nx + 1, inner]),
            (ylo.at[i], ps.at[i, mid, pl.ds(0, ROWS)]),
            (yhi.at[i], ps.at[i, mid, pl.ds(ROWS + ny, ROWS)]),
        ]
    pairs += [
        (pv, pvs), (old, olds),
        (t.at[0], txs.at[pl.ds(0, nx)]), (xt, txs.at[nx]),
        (t.at[1], tys.at[:, pl.ds(0, ny)]), (yt, tys.at[:, pl.ds(ny, ROWS)]),
        (t.at[2], tzs),
        (u.at[0], uxs.at[:, pl.ds(0, nx)]), (xu, uxs.at[:, nx]),
        (u.at[1], uys.at[:, :, pl.ds(0, ny)]), (yu, uys.at[:, :, pl.ds(ny, ROWS)]),
        (u.at[2], uzs),
    ]
    copies = [pltpu.make_async_copy(a, b, in_sem.at[k]) for k, (a, b) in enumerate(pairs)]
    for copy in copies:
        copy.start()
    for copy in copies:
        copy.wait()

    gx, gy = lax.axis_index("gx"), lax.axis_index("gy")

    @pl.when(gx == 0)
    def _():
        txs[0] = jnp.zeros((ny, nz), jnp.float32)

    @pl.when(gx == lax.axis_size("gx") - 1)
    def _():
        txs[nx] = jnp.zeros((ny, nz), jnp.float32)

    @pl.when(gy == 0)
    def _():
        tys[:, 0:1] = jnp.zeros((nx, 1, nz), jnp.float32)

    @pl.when(gy == lax.axis_size("gy") - 1)
    def _():
        tys[:, ny : ny + 1] = jnp.zeros((nx, 1, nz), jnp.float32)

    side_s[:, 0:ROWS] = jnp.zeros((nx // 2, ROWS, nz), jnp.float32)
    side_s[:, ny + ROWS :] = jnp.zeros((nx // 2, ROWS, nz), jnp.float32)

    lane = lax.broadcasted_iota(jnp.int32, (ROWS, nz), 1)
    odd = lax.broadcasted_iota(jnp.int32, (ROWS, nz), 0) % 2 == 1
    flat, depth = (0.0, 0.0, 0.0), (0.1, 0.08, 0.02)
    outs = ((res_v, res_o), (diag_v, diag_o), (low_v, low_o), (up_v, up_o), (rows_v, rows_o), (pro_v, pro_o))

    def out_copies(j):
        made = []
        rows = pl.ds(pl.multiple_of(j * ROWS, ROWS), ROWS)
        for k, (v, o) in enumerate(outs):
            lead = (slice(None),) * (len(v.shape) - 2)
            made.append(pltpu.make_async_copy(v.at[lead + (rows,)], o.at[lead + (rows,)], out_sem.at[j, k]))
        return made

    def step(j, carry):
        start = pl.multiple_of(j * ROWS, ROWS)
        rows = pl.ds(start, ROWS)
        here = pl.ds(pl.multiple_of(start + ROWS, ROWS), ROWS)
        before = pl.ds(start + ROWS - 1, ROWS)
        after = pl.ds(start + ROWS + 1, ROWS)
        following = pl.ds(start + 1, ROWS)

        def states(x, where):
            return [ps[i, x, where] for i in range(3)]

        def x_face(x, low, high):
            return face(low, high, txs[x, rows], [uxs[a, x, rows] for a in range(3)], flat)

        below, centre = cell(*states(0, here)), cell(*states(1, here))
        x_low = x_face(0, below, centre)
        agg = [None] * (nx // 2)
        side = [None] * (nx // 2)

        def add(items, place, value):
            items[place] = value if items[place] is None else items[place] + value

        for x in range(nx):
            above = cell(*states(x + 2, here))
            x_up = x_face(x + 1, centre, above)
            y_low = face(
                cell(*states(x + 1, before)), centre, tys[x, rows],
                [uys[a, x, rows] for a in range(3)], flat,
            )
            y_up = face(
                centre, cell(*states(x + 1, after)), tys[x, following],
                [uys[a, x, following] for a in range(3)], flat,
            )
            under = cell(*[pltpu.roll(centre[n], 1, 1) for n in ("p", "sw", "sg")])
            z_t = jnp.where(lane > 0, tzs[x, rows], 0.0)
            z_low = face(under, centre, z_t, [uzs[a, x, rows] for a in range(3)], depth)
            z_up = [[pltpu.roll(v, nz - 1, 1) for v in part] for part in z_low]
            lows, ups = (x_low, y_low, z_low), (x_up, y_up, z_up)

            c = centre
            pore = pvs[x, rows]
            phi = pore + 0.02 * pore * c["p"]
            dphi = 0.02 * pore
            water, oil = c["bw"] * c["sw"], c["sob"]
            gas = c["p"] * c["sg"] + c["rs"] * oil
            pob = phi * c["bo"]
            rob = c["rs"] * pob
            acc = [
                dphi * water + 0.05 * phi * c["sw"],
                phi * c["bw"],
                dphi * oil + 0.1 * phi * c["so"],
                -pob,
                dphi * gas + phi * (c["sg"] + 0.3 * oil + 0.1 * c["rs"] * c["so"]),
                -rob,
                phi * c["p"] - rob,
            ]
            acc = [2.0 * v for v in acc]
            mass = (phi * water, phi * oil, phi * gas)
            residual = []
            for k in range(3):
                r = 2.0 * (mass[k] - olds[k, x, rows])
                for d in range(3):
                    r = r - lows[d][0][k] + ups[d][0][k]
                res_v[k, x, rows] = r
                residual.append(r)
            diag = []
            for k in range(7):
                v = acc[k]
                for d in range(3):
                    v = v - lows[d][2][k] + ups[d][1][k]
                diag.append(v)
            put(diag_v, (), x, rows, diag)
            for d in range(3):
                put(low_v, (d,), x, rows, lows[d][1], -1.0)
                put(up_v, (d,), x, rows, ups[d][2])

            weight = (1.0 / c["bw"], 1.0 / c["bo"] - 0.3, 1.0 / c["p"])
            p_diag = column(weight, diag)
            p_low = [-column(weight, lows[d][1]) for d in range(3)]
            p_up = [column(weight, ups[d][2]) for d in range(3)]
            divisor = jnp.abs(p_diag) + column(weight, acc)
            for v in p_low + p_up:
                divisor = divisor + jnp.abs(v)
            scale = (2.0 / 3.0) / divisor
            for k, v in enumerate([p_diag] + p_low + p_up):
                rows_v[k, x, rows] = v
            y_same = jnp.where(odd, p_low[1], p_up[1])
            y_low_other = jnp.where(odd, 0.0, p_low[1])
            y_up_other = jnp.where(odd, p_up[1], 0.0)
            x_same, x_other = (p_low[0], p_up[0]) if x % 2 else (p_up[0], p_low[0])
            own = 1.0 - scale * (p_diag + x_same + y_same)
            minus = -scale
            w_x = minus * x_other
            w_yl, w_yu = minus * y_low_other, minus * y_up_other
            w_zl, w_zu = minus * p_low[2], minus * p_up[2]
            none = jnp.zeros_like(own)
            w_xl, w_xu = (none, w_x) if x % 2 else (w_x, none)
            for k, v in enumerate((own, w_xl, w_yl, w_zl, w_xu, w_yu, w_zu)):
                pro_v[k, x, rows] = v

            reduced = weight[0] * residual[0] + weight[1] * residual[1] + weight[2] * residual[2]
            local = own * reduced + pltpu.roll(w_zl * reduced, nz - 1, 1) + pltpu.roll(w_zu * reduced, 1, 1)
            add(agg, x // 2, local)
            add(side, x // 2, (w_yl + w_yu) * reduced)
            share = w_x * reduced
            if x == 0:
                own_s[nx // 2, rows] = share
            elif x == nx - 1:
                own_s[nx // 2 + 1, rows] = share
            else:
                add(agg, (x + 1) // 2 if x % 2 else (x - 1) // 2, share)
            x_low, centre = x_up, above
        for a in range(nx // 2):
            own_s[a, rows] = agg[a]
            side_s[a, here] = side[a]
        for copy in out_copies(j):
            copy.start()
        return carry

    lax.fori_loop(0, steps, step, 0)

    half = ny // 2
    for a in range(nx // 2):
        coarse_o[a] = (
            own_s[a, pl.ds(0, half, stride=2)]
            + own_s[a, pl.ds(1, half, stride=2)]
            + side_s[a, pl.ds(ROWS + 2, half, stride=2)]
            + side_s[a, pl.ds(ROWS - 1, half, stride=2)]
        )
        sy_o[0, a : a + 1] = side_s[a, ROWS : ROWS + 1]
        sy_o[1, a : a + 1] = side_s[a, ROWS + ny - 1 : ROWS + ny]
    for s in range(2):
        sx_o[s] = own_s[nx // 2 + s, pl.ds(0, half, stride=2)] + own_s[nx // 2 + s, pl.ds(1, half, stride=2)]

    def finish(j, carry):
        for copy in out_copies(j):
            copy.wait()
        return carry

    lax.fori_loop(0, steps, finish, 0)


def share_kernel(coarse, sx, sy, out, gx_in, gy_in, send, recv):
    ax, half, nz = coarse.shape
    (_, xl, has_xl), (_, xh, has_xh), (_, yl, has_yl), (_, yh, has_yh) = neighbours()
    meet()
    routes = (
        (sx.at[0], gx_in.at[0], "gx", xl, has_xl, has_xh),
        (sx.at[1], gx_in.at[1], "gx", xh, has_xh, has_xl),
        (sy.at[0], gy_in.at[0], "gy", yl, has_yl, has_yh),
        (sy.at[1], gy_in.at[1], "gy", yh, has_yh, has_yl),
    )
    copies = []
    for k, (source, target, axis, other, sends, gets) in enumerate(routes):
        copy = pltpu.make_async_remote_copy(
            src_ref=source, dst_ref=target, send_sem=send.at[k], recv_sem=recv.at[k],
            device_id={axis: other}, device_id_type=MESH,
        )
        copies.append(copy)

        @pl.when(sends)
        def _():
            copy.start()

    out[...] = coarse[...]
    for k, (source, target, axis, other, sends, gets) in enumerate(routes):
        copy = copies[k]

        @pl.when(gets)
        def _():
            copy.wait_recv()
            if k == 0:
                out[ax - 1] += gx_in[0]
            elif k == 1:
                out[0] += gx_in[1]
            else:
                place = half - 1 if k == 2 else 0
                for a in range(ax):
                    out[a, place : place + 1] += gy_in[k - 2, a : a + 1]

        @pl.when(sends)
        def _():
            copy.wait_send()


def body(pressure, sat_water, sat_gas, pore_volume, mass_old, transmissibility, upwind):
    nx, ny, nz = pressure.shape
    f32, i32 = jnp.float32, jnp.int32
    anywhere = pl.BlockSpec(memory_space=pltpu.HBM)
    in_vmem = pl.BlockSpec(memory_space=pltpu.VMEM)
    shape = jax.ShapeDtypeStruct
    halos = pl.pallas_call(
        halo_kernel,
        out_shape=[
            shape((3, ny, nz), f32), shape((3, ny, nz), f32), shape((ny, nz), f32), shape((3, ny, nz), i32),
            shape((3, nx, ROWS, nz), f32), shape((3, nx, ROWS, nz), f32), shape((nx, ROWS, nz), f32),
            shape((3, nx, ROWS, nz), i32),
        ],
        in_specs=[anywhere] * 5,
        out_specs=[anywhere] * 8,
        scratch_shapes=[pltpu.SemaphoreType.DMA((16,)), pltpu.SemaphoreType.DMA((16,))],
        compiler_params=pltpu.CompilerParams(collective_id=0, has_side_effects=True),
        name="halo",
    )(pressure, sat_water, sat_gas, transmissibility, upwind)
    grid = (nx, ny, nz)
    lead = ((3,), (9,), (3, 9), (3, 9), (7,), (7,))
    results = pl.pallas_call(
        main_kernel,
        out_shape=[shape(k + grid, f32) for k in lead]
        + [shape((nx // 2, ny // 2, nz), f32), shape((2, ny // 2, nz), f32), shape((2, nx // 2, nz), f32)],
        in_specs=[anywhere] * 15,
        out_specs=[anywhere] * 6 + [in_vmem] * 3,
        scratch_shapes=[
            pltpu.VMEM((3, nx + 2, ny + 2 * ROWS, nz), f32),
            pltpu.VMEM(grid, f32),
            pltpu.VMEM((3,) + grid, f32),
            pltpu.VMEM((nx + 1, ny, nz), f32),
            pltpu.VMEM((nx, ny + ROWS, nz), f32),
            pltpu.VMEM(grid, f32),
            pltpu.VMEM((3, nx + 1, ny, nz), i32),
            pltpu.VMEM((3, nx, ny + ROWS, nz), i32),
            pltpu.VMEM((3,) + grid, i32),
        ]
        + [pltpu.VMEM(k + grid, f32) for k in lead]
        + [
            pltpu.VMEM((nx // 2 + 2, ny, nz), f32),
            pltpu.VMEM((nx // 2, ny + 2 * ROWS, nz), f32),
            pltpu.SemaphoreType.DMA((27,)),
            pltpu.SemaphoreType.DMA((ny // ROWS, 6)),
        ],
        compiler_params=pltpu.CompilerParams(vmem_limit_bytes=62 * 2**20),
        name="assemble",
    )(pressure, sat_water, sat_gas, pore_volume, mass_old, transmissibility, upwind, *halos)
    *blocks, coarse, sx, sy = results
    coarse = pl.pallas_call(
        share_kernel,
        out_shape=shape(coarse.shape, f32),
        in_specs=[in_vmem] * 3,
        out_specs=in_vmem,
        scratch_shapes=[
            pltpu.VMEM(sx.shape, f32), pltpu.VMEM(sy.shape, f32),
            pltpu.SemaphoreType.DMA((4,)), pltpu.SemaphoreType.DMA((4,)),
        ],
        compiler_params=pltpu.CompilerParams(collective_id=1, has_side_effects=True),
        name="shares",
    )(coarse, sx, sy)
    return (*blocks, coarse)


def solution(mesh):
    cells = P("gx", "gy", None)
    one = P(None, "gx", "gy", None)
    two = P(None, None, "gx", "gy", None)
    return jax.shard_map(
        body,
        mesh=mesh,
        in_specs=(cells, cells, cells, cells, one, one, two),
        out_specs=(one, one, two, two, one, one, cells),
        check_vma=False,
    )
```

```python
import jax
import jax.numpy as jnp
from jax import lax
from jax.experimental import pallas as pl
from jax.experimental.pallas import tpu as pltpu
from jax.sharding import PartitionSpec as P

MESH = pl.DeviceIdType.MESH
ROWS = 8
CHUNK = 16
LIMIT = 24 * 2**20
PLACES = (0, 1, 3, 4, 6, 7, 8)


def neighbours():
    found = []
    for axis in ("gx", "gy"):
        here, size = lax.axis_index(axis), lax.axis_size(axis)
        found.append((axis, here - 1, here > 0))
        found.append((axis, here + 1, here < size - 1))
    return found


def meet():
    barrier = pltpu.get_barrier_semaphore()
    for axis, other, there in neighbours():

        @pl.when(there)
        def _():
            pl.semaphore_signal(barrier, inc=1, device_id={axis: other}, device_id_type=MESH)

    peers = sum(there.astype(jnp.int32) for _, _, there in neighbours())
    pl.semaphore_wait(barrier, peers)


def cell(p, sw, sg):
    so = 1.0 - sw - sg
    bw = 1.0 + 0.05 * p
    bo = 1.0 + 0.1 * p
    ww, oo, gg = sw * sw, so * so, 5.0 * (sg * sg)
    sob = so * bo
    return dict(
        p=p, sw=sw, sg=sg, so=so, bw=bw, bo=bo, sob=sob, rs=0.3 * p,
        m=(2.0 * ww * bw, 0.5 * so * sob, gg * p),
        mp=(0.1 * ww, 0.05 * oo, gg),
        ms=(4.0 * sw * bw, -sob, 10.0 * sg * p),
    )


def face(low, high, t, flags, heads):
    drop = low["p"] - high["p"]
    ups = [flag > 0 for flag in flags]
    flow, by_low, by_high = [], [], []
    for a in range(3):
        drive = t * (drop + heads[a]) if heads[a] else t * drop
        chosen = jnp.where(ups[a], low["m"][a], high["m"][a])
        moved = t * chosen
        flow.append(drive * chosen)
        from_low = jnp.where(ups[a], drive, 0.0)
        from_high = jnp.where(ups[a], 0.0, drive)
        by_low.append((from_low * low["mp"][a] + moved, from_low * low["ms"][a]))
        by_high.append((from_high * high["mp"][a] - moved, from_high * high["ms"][a]))
    solved = jnp.where(ups[1], low["rs"], high["rs"])
    fluxes = [flow[0], flow[1], flow[2] + solved * flow[1]]
    third = 0.3 * flow[1]
    extra_low = jnp.where(ups[1], third, 0.0)
    extra_high = jnp.where(ups[1], 0.0, third)
    out = []
    for (w, o, g), extra in ((by_low, extra_low), (by_high, extra_high)):
        carried = solved * o[1]
        out.append([w[0], w[1], o[0], o[1], g[0] + solved * o[0] + extra, carried, g[1] + carried])
    return fluxes, out[0], out[1]


def column(weight, entries):
    return weight[0] * entries[0] + weight[1] * entries[2] + weight[2] * entries[4]


def put(ref, lead, x, rows, entries, sign=1.0):
    for place, entry in zip(PLACES, entries):
        ref[lead + (place, x, rows)] = entry if sign > 0 else -entry
    ref[lead + (2, x, rows)] = jnp.zeros_like(entries[0])
    ref[lead + (5, x, rows)] = entries[3] if sign > 0 else -entries[3]


def main_kernel(
    p, sw, sg, pv, old, t, u,
    res_v, diag_v, low_v, up_v, rows_v, pro_v, coarse_o,
    ps, pvs, olds, txs, tys, tzs, uxs, uys, uzs,
    own_s, side_s, sx, sy, gx_in, gy_in,
    in_sem, xs_sem, xr_sem, ys_sem, yr_sem, share_s, share_r,
):
    nx, ny, nz = p.shape
    chunks = ny // CHUNK
    inner = pl.ds(ROWS, ny)
    mid = pl.ds(1, nx)
    states_in = (p, sw, sg)
    pairs = [(s, ps.at[i, mid, inner]) for i, s in enumerate(states_in)]
    pairs += [
        (pv, pvs), (old, olds), (t.at[0], txs.at[pl.ds(0, nx)]), (t.at[1], tys.at[:, pl.ds(0, ny)]),
        (t.at[2], tzs), (u.at[0], uxs.at[:, pl.ds(0, nx)]), (u.at[1], uys.at[:, :, pl.ds(0, ny)]),
        (u.at[2], uzs),
    ]
    local = [pltpu.make_async_copy(a, b, in_sem.at[k]) for k, (a, b) in enumerate(pairs)]
    for copy in local:
        copy.start()

    (_, xl, has_xl), (_, xh, has_xh), (_, yl, has_yl), (_, yh, has_yh) = neighbours()

    def remote(pairs, send, recv, axis, other, base):
        return [
            pltpu.make_async_remote_copy(
                src_ref=a, dst_ref=b, send_sem=send(base + k), recv_sem=recv(base + k),
                device_id={axis: other}, device_id_type=MESH,
            )
            for k, (a, b) in enumerate(pairs)
        ]

    def x_copies(c):
        begin = pl.multiple_of(c * CHUNK, CHUNK)
        rows = pl.ds(begin, CHUNK)
        put_rows = pl.ds(pl.multiple_of(begin + ROWS, ROWS), CHUNK)
        up = [(s.at[nx - 1, rows], ps.at[i, 0, put_rows]) for i, s in enumerate(states_in)]
        down = [(s.at[0, rows], ps.at[i, nx + 1, put_rows]) for i, s in enumerate(states_in)]
        down += [(t.at[0, 0, rows], txs.at[nx, rows]), (u.at[0, :, 0, rows], uxs.at[:, nx, rows])]
        send, recv = (lambda k: xs_sem.at[c, k]), (lambda k: xr_sem.at[c, k])
        return remote(up, send, recv, "gx", xh, 0), remote(down, send, recv, "gx", xl, 3)

    first, last, beyond = pl.ds(0, ROWS), pl.ds(ny - ROWS, ROWS), pl.ds(ny + ROWS, ROWS)
    up = [(s.at[:, last], ps.at[i, mid, first]) for i, s in enumerate(states_in)]
    down = [(s.at[:, first], ps.at[i, mid, beyond]) for i, s in enumerate(states_in)]
    down += [(t.at[1, :, first], tys.at[:, pl.ds(ny, ROWS)]), (u.at[1, :, :, first], uys.at[:, :, pl.ds(ny, ROWS)])]
    y_up = remote(up, lambda k: ys_sem.at[k], lambda k: yr_sem.at[k], "gy", yh, 0)
    y_down = remote(down, lambda k: ys_sem.at[k], lambda k: yr_sem.at[k], "gy", yl, 3)

    def when(there, copies, what):
        @pl.when(there)
        def _():
            for copy in copies:
                getattr(copy, what)()

    meet()

    def begin(c, carry):
        x_up, x_down = x_copies(c)
        when(has_xl, x_down, "start")
        when(has_xh, x_up, "start")
        return carry

    lax.fori_loop(0, 1, begin, 0)
    when(has_yl, y_down, "start")
    when(has_yh, y_up, "start")
    lax.fori_loop(1, chunks, begin, 0)
    none_there = jnp.logical_not

    @pl.when(none_there(has_xl))
    def _():
        ps[:, 0] = jnp.zeros((3, ny + 2 * ROWS, nz), jnp.float32)

    @pl.when(none_there(has_xh))
    def _():
        ps[:, nx + 1] = jnp.zeros((3, ny + 2 * ROWS, nz), jnp.float32)
        txs[nx] = jnp.zeros((ny, nz), jnp.float32)
        uxs[:, nx] = jnp.zeros((3, ny, nz), jnp.int32)

    @pl.when(none_there(has_yl))
    def _():
        ps[:, 1 : nx + 1, 0:ROWS] = jnp.zeros((3, nx, ROWS, nz), jnp.float32)

    @pl.when(none_there(has_yh))
    def _():
        ps[:, 1 : nx + 1, ny + ROWS :] = jnp.zeros((3, nx, ROWS, nz), jnp.float32)
        tys[:, ny:] = jnp.zeros((nx, ROWS, nz), jnp.float32)
        uys[:, :, ny:] = jnp.zeros((3, nx, ROWS, nz), jnp.int32)

    for copy in local:
        copy.wait()

    @pl.when(none_there(has_xl))
    def _():
        txs[0] = jnp.zeros((ny, nz), jnp.float32)

    @pl.when(none_there(has_yl))
    def _():
        tys[:, 0:1] = jnp.zeros((nx, 1, nz), jnp.float32)

    when(has_yh, y_down, "wait_recv")
    when(has_yl, y_up, "wait_recv")

    side_s[:, 0:ROWS] = jnp.zeros((nx // 2, ROWS, nz), jnp.float32)
    side_s[:, ny + ROWS :] = jnp.zeros((nx // 2, ROWS, nz), jnp.float32)

    lane = lax.broadcasted_iota(jnp.int32, (ROWS, nz), 1)
    odd = lax.broadcasted_iota(jnp.int32, (ROWS, nz), 0) % 2 == 1
    flat, depth = (0.0, 0.0, 0.0), (0.1, 0.08, 0.02)
    def step(j, carry):
        start = pl.multiple_of(j * ROWS, ROWS)
        rows = pl.ds(start, ROWS)
        here = pl.ds(pl.multiple_of(start + ROWS, ROWS), ROWS)
        before = pl.ds(start + ROWS - 1, ROWS)
        after = pl.ds(start + ROWS + 1, ROWS)
        following = pl.ds(start + 1, ROWS)

        def states(x, where):
            return [ps[i, x, where] for i in range(3)]

        def x_face(x, low, high):
            return face(low, high, txs[x, rows], [uxs[a, x, rows] for a in range(3)], flat)

        below, centre = cell(*states(0, here)), cell(*states(1, here))
        x_low = x_face(0, below, centre)
        agg = [None] * (nx // 2)
        side = [None] * (nx // 2)

        def add(items, place, value):
            items[place] = value if items[place] is None else items[place] + value

        for x in range(nx):
            above = cell(*states(x + 2, here))
            x_up = x_face(x + 1, centre, above)
            y_low = face(
                cell(*states(x + 1, before)), centre, tys[x, rows],
                [uys[a, x, rows] for a in range(3)], flat,
            )
            y_up = face(
                centre, cell(*states(x + 1, after)), tys[x, following],
                [uys[a, x, following] for a in range(3)], flat,
            )
            under = cell(*[pltpu.roll(centre[n], 1, 1) for n in ("p", "sw", "sg")])
            z_t = jnp.where(lane > 0, tzs[x, rows], 0.0)
            z_low = face(under, centre, z_t, [uzs[a, x, rows] for a in range(3)], depth)
            z_up = [[pltpu.roll(v, nz - 1, 1) for v in part] for part in z_low]
            lows, ups = (x_low, y_low, z_low), (x_up, y_up, z_up)

            c = centre
            pore = pvs[x, rows]
            phi = pore + 0.02 * pore * c["p"]
            dphi = 0.02 * pore
            water, oil = c["bw"] * c["sw"], c["sob"]
            gas = c["p"] * c["sg"] + c["rs"] * oil
            pob = phi * c["bo"]
            rob = c["rs"] * pob
            acc = [
                dphi * water + 0.05 * phi * c["sw"],
                phi * c["bw"],
                dphi * oil + 0.1 * phi * c["so"],
                -pob,
                dphi * gas + phi * (c["sg"] + 0.3 * oil + 0.1 * c["rs"] * c["so"]),
                -rob,
                phi * c["p"] - rob,
            ]
            acc = [2.0 * v for v in acc]
            mass = (phi * water, phi * oil, phi * gas)
            residual = []
            for k in range(3):
                r = 2.0 * (mass[k] - olds[k, x, rows])
                for d in range(3):
                    r = r - lows[d][0][k] + ups[d][0][k]
                res_v[k, x, rows] = r
                residual.append(r)
            diag = []
            for k in range(7):
                v = acc[k]
                for d in range(3):
                    v = v - lows[d][2][k] + ups[d][1][k]
                diag.append(v)
            put(diag_v, (), x, rows, diag)
            for d in range(3):
                put(low_v, (d,), x, rows, lows[d][1], -1.0)
                put(up_v, (d,), x, rows, ups[d][2])

            weight = (1.0 / c["bw"], 1.0 / c["bo"] - 0.3, 1.0 / c["p"])
            p_diag = column(weight, diag)
            p_low = [-column(weight, lows[d][1]) for d in range(3)]
            p_up = [column(weight, ups[d][2]) for d in range(3)]
            divisor = jnp.abs(p_diag) + column(weight, acc)
            for v in p_low + p_up:
                divisor = divisor + jnp.abs(v)
            scale = (2.0 / 3.0) / divisor
            for k, v in enumerate([p_diag] + p_low + p_up):
                rows_v[k, x, rows] = v
            y_same = jnp.where(odd, p_low[1], p_up[1])
            y_low_other = jnp.where(odd, 0.0, p_low[1])
            y_up_other = jnp.where(odd, p_up[1], 0.0)
            x_same, x_other = (p_low[0], p_up[0]) if x % 2 else (p_up[0], p_low[0])
            own = 1.0 - scale * (p_diag + x_same + y_same)
            minus = -scale
            w_x = minus * x_other
            w_yl, w_yu = minus * y_low_other, minus * y_up_other
            w_zl, w_zu = minus * p_low[2], minus * p_up[2]
            none = jnp.zeros_like(own)
            w_xl, w_xu = (none, w_x) if x % 2 else (w_x, none)
            for k, v in enumerate((own, w_xl, w_yl, w_zl, w_xu, w_yu, w_zu)):
                pro_v[k, x, rows] = v

            reduced = weight[0] * residual[0] + weight[1] * residual[1] + weight[2] * residual[2]
            local = own * reduced + pltpu.roll(w_zl * reduced, nz - 1, 1) + pltpu.roll(w_zu * reduced, 1, 1)
            add(agg, x // 2, local)
            add(side, x // 2, (w_yl + w_yu) * reduced)
            share = w_x * reduced
            if x == 0:
                own_s[nx // 2, rows] = share
            elif x == nx - 1:
                own_s[nx // 2 + 1, rows] = share
            else:
                add(agg, (x + 1) // 2 if x % 2 else (x - 1) // 2, share)
            x_low, centre = x_up, above
        for a in range(nx // 2):
            own_s[a, rows] = agg[a]
            side_s[a, here] = side[a]
        return carry

    per = CHUNK // ROWS

    def chunk(c, carry):
        x_up, x_down = x_copies(c)
        when(has_xl, x_up, "wait_recv")
        when(has_xh, x_down, "wait_recv")
        return lax.fori_loop(c * per, (c + 1) * per, step, carry)

    lax.fori_loop(0, chunks, chunk, 0)

    half = ny // 2
    for s in range(2):
        sx[s] = own_s[nx // 2 + s, pl.ds(0, half, stride=2)] + own_s[nx // 2 + s, pl.ds(1, half, stride=2)]
    for a in range(nx // 2):
        sy[0, a : a + 1] = side_s[a, ROWS : ROWS + 1]
        sy[1, a : a + 1] = side_s[a, ROWS + ny - 1 : ROWS + ny]
    routes = (
        (sx.at[0], gx_in.at[0], "gx", xl, has_xl, has_xh),
        (sx.at[1], gx_in.at[1], "gx", xh, has_xh, has_xl),
        (sy.at[0], gy_in.at[0], "gy", yl, has_yl, has_yh),
        (sy.at[1], gy_in.at[1], "gy", yh, has_yh, has_yl),
    )
    shares = []
    for k, (source, target, axis, other, sends, gets) in enumerate(routes):
        copy = remote([(source, target)], lambda n: share_s.at[n], lambda n: share_r.at[n], axis, other, k)
        shares.append(copy)
        when(sends, copy, "start")
    for a in range(nx // 2):
        coarse_o[a] = (
            own_s[a, pl.ds(0, half, stride=2)]
            + own_s[a, pl.ds(1, half, stride=2)]
            + side_s[a, pl.ds(ROWS + 2, half, stride=2)]
            + side_s[a, pl.ds(ROWS - 1, half, stride=2)]
        )
    when(has_yl, y_down, "wait_send")
    when(has_yh, y_up, "wait_send")

    def sent(c, carry):
        x_up, x_down = x_copies(c)
        when(has_xl, x_down, "wait_send")
        when(has_xh, x_up, "wait_send")
        return carry

    lax.fori_loop(0, chunks, sent, 0)
    for k, (source, target, axis, other, sends, gets) in enumerate(routes):
        when(gets, shares[k], "wait_recv")

        @pl.when(gets)
        def _():
            if k == 0:
                coarse_o[nx // 2 - 1] += gx_in[0]
            elif k == 1:
                coarse_o[0] += gx_in[1]
            else:
                place = half - 1 if k == 2 else 0
                for a in range(nx // 2):
                    coarse_o[a, place : place + 1] += gy_in[k - 2, a : a + 1]

        when(sends, shares[k], "wait_send")


def store_kernel(*refs):
    count = len(refs) // 2
    sem = refs[-1]
    copies = [pltpu.make_async_copy(refs[k], refs[count + k], sem.at[k]) for k in range(count)]
    for copy in copies:
        copy.start()
    for copy in copies:
        copy.wait()


def body(pressure, sat_water, sat_gas, pore_volume, mass_old, transmissibility, upwind):
    nx, ny, nz = pressure.shape
    f32, i32 = jnp.float32, jnp.int32
    anywhere = pl.BlockSpec(memory_space=pltpu.HBM)
    in_vmem = pl.BlockSpec(memory_space=pltpu.VMEM)
    shape = jax.ShapeDtypeStruct
    grid = (nx, ny, nz)
    lead = ((3,), (9,), (3, 9), (3, 9), (7,), (7,))
    outs = [shape(k + grid, f32) for k in lead] + [shape((nx // 2, ny // 2, nz), f32)]
    dma = pltpu.SemaphoreType.DMA
    results = pl.pallas_call(
        main_kernel,
        out_shape=[pltpu.VMEM(o.shape, o.dtype) for o in outs],
        in_specs=[anywhere] * 7,
        out_specs=[in_vmem] * 7,
        scratch_shapes=[
            pltpu.VMEM((3, nx + 2, ny + 2 * ROWS, nz), f32),
            pltpu.VMEM(grid, f32),
            pltpu.VMEM((3,) + grid, f32),
            pltpu.VMEM((nx + 1, ny, nz), f32),
            pltpu.VMEM((nx, ny + ROWS, nz), f32),
            pltpu.VMEM(grid, f32),
            pltpu.VMEM((3, nx + 1, ny, nz), i32),
            pltpu.VMEM((3, nx, ny + ROWS, nz), i32),
            pltpu.VMEM((3,) + grid, i32),
            pltpu.VMEM((nx // 2 + 2, ny, nz), f32),
            pltpu.VMEM((nx // 2, ny + 2 * ROWS, nz), f32),
            pltpu.VMEM((2, ny // 2, nz), f32), pltpu.VMEM((2, nx // 2, nz), f32),
            pltpu.VMEM((2, ny // 2, nz), f32), pltpu.VMEM((2, nx // 2, nz), f32),
            dma((11,)), dma((ny // CHUNK, 8)), dma((ny // CHUNK, 8)), dma((8,)), dma((8,)), dma((4,)), dma((4,)),
        ],
        compiler_params=pltpu.CompilerParams(
            collective_id=0, has_side_effects=True, vmem_limit_bytes=LIMIT
        ),
        name="assemble",
    )(*[
        pltpu.with_memory_space_constraint(v, pltpu.HBM)
        for v in (pressure, sat_water, sat_gas, pore_volume, mass_old, transmissibility, upwind)
    ])
    return pl.pallas_call(
        store_kernel,
        out_shape=outs,
        in_specs=[in_vmem] * 7,
        out_specs=[anywhere] * 7,
        scratch_shapes=[dma((7,))],
        compiler_params=pltpu.CompilerParams(vmem_limit_bytes=LIMIT),
        name="store",
    )(*results)


def solution(mesh):
    cells = P("gx", "gy", None)
    one = P(None, "gx", "gy", None)
    two = P(None, None, "gx", "gy", None)
    return jax.shard_map(
        body,
        mesh=mesh,
        in_specs=(cells, cells, cells, cells, one, one, two),
        out_specs=(one, one, two, two, one, one, cells),
        check_vma=False,
    )
```
